32 devices in a mesh: groups: 1, sample: 32 (over z, y, x, core).
Axes of the slice: x: 2, y: 2, z: 4, core: 2. Of those that a mesh axis runs over, the one named last changes fastest.
Arguments:
- hidden: bfloat16 [32, 256, 14336], P(('groups', 'sample')), may hold values from -6 to 6
- cotangent: bfloat16 [32, 256, 4096], P(('groups', 'sample')), may hold values from -6 to 6
- loss_mask: int32 [32, 256], P(('groups', 'sample')), may hold values 0 or 1
- project_hidden: bfloat16 [14336, 64], replicated, may hold values from -0.046875 to 0.046875
- project_model: bfloat16 [4096, 64], replicated, may hold values from -0.09375 to 0.09375
- queries: int32 [32], P('groups'), may hold values from 0 to 31, as said below
Outputs:
- projected: float32 [32, 4096], P(('groups', 'sample'))
- scores: float32 [32, 32], P(('groups', 'sample'))
The draws below stay inside these ranges and needn't reach their ends.
Inputs may be any that keep to these rules, and one draw needn't show every extreme that they name: `queries`: 32 distinct indices; the last sequence of the block is always among them.
All inputs are finite; a program needn't handle non-finite values. No bound on the sum of `loss_mask` on one device may be relied on, other than what follows from the above.
Results may differ from the reference program's by a relative error of at most 0.0003.
Values sent between devices are 32-bit elements; how exact they have to be, the bound alone decides.
A program may use at most 64 MiB of HBM per device.

```python
import jax
import jax.numpy as jnp
from jax import lax

D = 4096
FF = 14336
RANK = 64
SEQ = 256
QUERIES = 32
SAMPLES = 32


def draw_queries(key, part):
    key = jax.random.fold_in(key, 7)
    first, second = jax.random.split(key)
    others = jax.random.permutation(first, SAMPLES - 1)[:QUERIES - 1].astype(jnp.int32)
    full = jnp.concatenate([others, jnp.array([SAMPLES - 1], dtype=jnp.int32)])
    return jax.random.permutation(second, full).astype(jnp.int32)


def touch_ends(values, own_key, low, top_value):
    longest = values.shape.index(max(values.shape))
    spots = []
    for shift in (0, 1):
        where = [jax.random.randint(jax.random.fold_in(own_key, axis), (), 0, length) for axis, length in enumerate(values.shape)]
        where[longest] = (where[longest] + shift) % values.shape[longest]
        spots.append(tuple(where))
    return values.at[spots[0]].set(low).at[spots[1]].set(top_value)


def levels(stream_key, shape, cuts, low, high):
    loudness, own = 1.0, jax.random.fold_in(stream_key, 6)
    for position, shards_of in cuts:
        heights = jnp.exp(jax.random.uniform(jax.random.fold_in(own, position), (shards_of,), jnp.float32, low / len(cuts), high / len(cuts)))
        loudness = loudness * jnp.repeat(heights, shape[position] // shards_of).reshape([-1 if axis == position else 1 for axis in range(len(shape))])
    return loudness


def normal_values(stream_key, extent, width, bound, cuts=(), kind=jnp.bfloat16):
    loudness = levels(stream_key, extent, cuts, -0.22, 0.18) if cuts else 1.0
    result = jax.random.normal(stream_key, extent, jnp.float32) * width * loudness
    return jnp.minimum(jnp.maximum(result, -bound), bound).astype(kind)


def setup_inputs(seed: int = 0, part: int = 0) -> dict:
    key_list = jax.random.split(jax.random.key(seed), 7)
    part_splits = jax.random.split(jax.random.fold_in(key_list[6], part), 7)
    hidden = normal_values(part_splits[0], (SAMPLES, SEQ, FF), 1.0, 6.0, ((0, 32),))
    cotangent = normal_values(part_splits[1], (SAMPLES, SEQ, D), 1.0, 6.0, ((0, 32),))
    loss_mask = touch_ends((jax.random.randint(part_splits[2], (SAMPLES, SEQ), 0, 8) < 7).astype(jnp.int32), jax.random.fold_in(part_splits[2], 1), 0, 1)
    project_hidden = normal_values(key_list[3], (FF, RANK), FF ** -0.5, 0.046875)
    project_model = normal_values(key_list[4], (D, RANK), D ** -0.5, 0.09375)
    queries = draw_queries(jax.random.fold_in(jax.random.fold_in(key_list[6], part), 71), part)
    return dict(hidden=hidden, cotangent=cotangent, loss_mask=loss_mask, project_hidden=project_hidden, project_model=project_model, queries=queries)


def damp(factor, counted):
    mean = factor / jnp.maximum(counted, 1.0)
    lam = 0.1 * jnp.trace(mean) / RANK + 1e-06
    return mean + lam * jnp.eye(RANK, dtype=jnp.float32)

def precondition(damped_in, damped_out, query_grads):
    nquery = query_grads.shape[0]
    lower_in = jnp.linalg.cholesky(damped_in)
    lower_out = jnp.linalg.cholesky(damped_out)
    stacked = jnp.transpose(query_grads, (1, 0, 2)).reshape(RANK, nquery * RANK)
    left = jax.scipy.linalg.cho_solve((lower_in, True), stacked)
    flipped = jnp.transpose(left.reshape(RANK, nquery, RANK), (2, 1, 0)).reshape(RANK, nquery * RANK)
    right = jax.scipy.linalg.cho_solve((lower_out, True), flipped)
    return jnp.transpose(right.reshape(RANK, nquery, RANK), (1, 2, 0)).reshape(nquery, RANK * RANK)

def one_sample(args):
    rows_hidden, rows_cot, rows_mask, project_hidden, project_model = args
    hidden_low = jnp.dot(rows_hidden.astype(jnp.float32), project_hidden.astype(jnp.float32), preferred_element_type=jnp.float32)
    maskf = rows_mask.astype(jnp.float32)[:, None]
    weighted = jnp.dot(rows_cot.astype(jnp.float32), project_model.astype(jnp.float32), preferred_element_type=jnp.float32) * maskf
    grad = jnp.dot(hidden_low.T, weighted, precision=lax.Precision.HIGHEST) / jnp.sqrt(jnp.float32(SEQ))
    factor_in = jnp.dot((hidden_low * maskf).T, hidden_low, precision=lax.Precision.HIGHEST)
    factor_out = jnp.dot(weighted.T, weighted, precision=lax.Precision.HIGHEST)
    return (grad.reshape(RANK * RANK), factor_in, factor_out, jnp.sum(maskf))

def reference(hidden, cotangent, loss_mask, project_hidden, project_model, queries):

    def step(index):
        return one_sample((hidden[index], cotangent[index], loss_mask[index], project_hidden, project_model))
    projected, fin, fout, counts = lax.map(step, jnp.arange(SAMPLES, dtype=jnp.int32))
    counted = jnp.sum(counts)
    damped_in = damp(lax.optimization_barrier(jnp.sum(fin, axis=0)), counted)
    damped_out = damp(lax.optimization_barrier(jnp.sum(fout, axis=0)), counted)
    picker = (queries[:, None] == jnp.arange(SAMPLES, dtype=jnp.int32)[None, :]).astype(jnp.float32)
    query_grads = jnp.dot(picker, projected, precision=lax.Precision.HIGHEST).reshape(QUERIES, RANK, RANK)
    precond = precondition(damped_in, damped_out, query_grads)
    scores = jnp.dot(projected, precond.T, precision=lax.Precision.HIGHEST) / RANK
    return (projected, scores)
```

```python
import functools

import jax
import jax.numpy as jnp
from jax import lax
from jax.experimental import pallas as pl
from jax.experimental.pallas import tpu as pltpu
from jax.sharding import PartitionSpec as P

MESH = pl.DeviceIdType.MESH
HIGHEST = lax.Precision.HIGHEST
PLANE = 8
NT = (((1,), (1,)), ((), ()))
SQUARINGS = 7


def exact(a, b):
    return jnp.dot(a, b, precision=HIGHEST, preferred_element_type=jnp.float32)


def inverses(factors):
    rank = factors.shape[0]
    row = lax.broadcasted_iota(jnp.int32, factors.shape, 0)
    lane = lax.broadcasted_iota(jnp.int32, factors.shape, 1)
    first = lane < rank
    diagonal = row == jnp.where(first, lane, lane - rank)

    def both(values):
        one = jnp.sum(jnp.where(first, values, 0.0), keepdims=True)
        two = jnp.sum(jnp.where(first, 0.0, values), keepdims=True)
        lane1 = lax.broadcasted_iota(jnp.int32, (1, 2 * rank), 1)
        return jnp.where(lane1 < rank, one, two)

    trace = both(jnp.where(diagonal, factors, 0.0))
    frob = jnp.sqrt(both(factors * factors))
    lam = 0.1 * trace / rank + 1e-06
    low, high = lam, lam + jnp.minimum(trace, frob) * 1.0001
    damped = jnp.where(diagonal, factors + lam, factors)

    def blocks(values):
        return jnp.concatenate(
            [jnp.where(first, values, 0.0), jnp.where(first, 0.0, values)], axis=0
        )

    eye = blocks(jnp.where(diagonal, 1.0, 0.0))
    damped = blocks(damped)
    scale = 2.0 / (low + high)
    rho = (high - low) / (high + low)
    x = eye * scale
    r = eye - damped * scale
    for _ in range(SQUARINGS):
        c = 2.0 / (2.0 - rho * rho)
        product = exact(jnp.concatenate([r, x], axis=0), r)
        x = (x + product[2 * rank :]) * c
        r = (1.0 - c) * eye + product[: 2 * rank] * c
        rho = rho * rho / (2.0 - rho * rho)
        yield None
    x = x + exact(x, eye - exact(damped, x))
    yield x


def kernel(
    n, chunks_h, chunks_c,
    hidden, cot, mask, proj_h, proj_m, queries,
    grads_out, scores_out,
    h_v, c_v, ph_v, pm_v, pair, fac, rs, red, zr, fs, g,
    in_sem, rs_send, rs_recv, z_send, z_recv, ag_send, ag_recv, g_send, g_recv,
):
    seq, ff = h_v.shape
    d = c_v.shape[1]
    rank = ph_v.shape[0]
    me = lax.axis_index("sample")
    high = n // PLANE
    hi, low = me // PLANE, me % PLANE

    def in_plane(t):
        return hi * PLANE + (low + t) % PLANE

    def in_column(t):
        return (hi + t) % high * PLANE + low

    loads = []
    step = d // chunks_c
    for i in range(chunks_c):
        cols = pl.ds(i * step, step)
        loads.append([(cot.at[0, :, cols], c_v.at[:, cols]), (proj_m.at[:, cols], pm_v.at[:, cols])])
    step = ff // chunks_h
    for i in range(chunks_h):
        cols = pl.ds(i * step, step)
        loads.append([(hidden.at[0, :, cols], h_v.at[:, cols]), (proj_h.at[:, cols], ph_v.at[:, cols])])
    copies = []
    for i, two in enumerate(loads):
        copies.append(
            [pltpu.make_async_copy(src, dst, in_sem.at[2 * i + j]) for j, (src, dst) in enumerate(two)]
        )
        for copy in copies[-1]:
            copy.start()

    barrier = pltpu.get_barrier_semaphore()
    partners = [in_plane(t) for t in range(1, PLANE)] + [in_column(t) for t in range(1, high)]
    for partner in partners:
        pl.semaphore_signal(barrier, inc=1, device_id={"sample": partner}, device_id_type=MESH)

    weighted = jnp.zeros((rank, seq), jnp.float32)
    step = d // chunks_c
    for i in range(chunks_c):
        for copy in copies[i]:
            copy.wait()
        cols = pl.ds(i * step, step)
        weighted += lax.dot_general(pm_v[:, cols], c_v[:, cols], NT, preferred_element_type=jnp.float32)
    hidden_low = jnp.zeros((rank, seq), jnp.float32)
    step = ff // chunks_h
    for i in range(chunks_h):
        for copy in copies[chunks_c + i]:
            copy.wait()
        cols = pl.ds(i * step, step)
        hidden_low += lax.dot_general(ph_v[:, cols], h_v[:, cols], NT, preferred_element_type=jnp.float32)

    maskf = mask[...].astype(jnp.float32)
    both = jnp.concatenate([hidden_low, weighted], axis=0) * maskf
    gram = lax.dot_general(both, both, NT, precision=HIGHEST, preferred_element_type=jnp.float32)
    row = lax.broadcasted_iota(jnp.int32, (rank, 2 * rank), 0)
    lane = lax.broadcasted_iota(jnp.int32, (rank, 2 * rank), 1)
    first = lane < rank
    factors = jnp.where(first, gram[:rank], gram[rank:])
    spare = (row == 1) & (lane == 0)
    count = jnp.sum(maskf, keepdims=True)
    fac[...] = jnp.where(spare, count, factors).reshape(fac.shape)

    pl.semaphore_wait(barrier, len(partners))

    def remote(src, dst, send, recv, partner):
        return pltpu.make_async_remote_copy(
            src_ref=src, dst_ref=dst, send_sem=send, recv_sem=recv,
            device_id={"sample": partner}, device_id_type=MESH,
        )

    started = []

    def start(copies):
        for copy in copies:
            copy.start()
        started.extend(copies)
        return copies

    to_plane = start([
        remote(fac.at[(low + t) % PLANE], rs.at[t - 1], rs_send.at[t - 1], rs_recv.at[t - 1], in_plane(t))
        for t in range(1, PLANE)
    ])

    grad = jnp.where(first, 0.0, gram[:rank]) * (1.0 / seq**0.5)
    twice = grad + pltpu.roll(grad, rank, 1)
    half = rank // 2
    place = hi + high * ((low // 4) % 2) + 2 * high * ((low // 2) % 2) + 4 * high * (low % 2)
    g[place] = jnp.where(first[:half], twice[:half], twice[half:])

    def g_copies(stage):
        if stage == 0:
            return [
                remote(g.at[place], g.at[place], g_send.at[t - 1], g_recv.at[t - 1], in_column(t))
                for t in range(1, high)
            ]
        held = high * 2 ** (stage - 1)
        bit = PLANE // 2**stage
        partner = me + (1 - 2 * ((me // bit) % 2)) * bit
        span = pl.ds(pl.multiple_of(place // held * held, held), held)
        sem = high - 2 + stage
        return [remote(g.at[span], g.at[span], g_send.at[sem], g_recv.at[sem], partner)]

    stages = [start(g_copies(0))]

    def next_stage():
        for copy in stages[-1]:
            copy.wait_recv()
        if len(stages) < 4:
            stages.append(start(g_copies(len(stages))))

    pair[...] = twice
    grads_out[...] = jnp.where(
        first[:half], pair[pl.ds(0, half, stride=2), :], pair[pl.ds(1, half, stride=2), :]
    )

    for copy in to_plane:
        copy.wait_recv()
    part = fac[low]
    for t in range(PLANE - 1):
        part += rs[t]
    red[...] = part
    to_column = start([
        remote(red, zr.at[t - 1], z_send.at[t - 1], z_recv.at[t - 1], in_column(t))
        for t in range(1, high)
    ])
    next_stage()
    for copy in to_column:
        copy.wait_recv()
    for t in range(high - 1):
        part += zr[t]
    fs[low] = part
    shares = start([
        remote(fs.at[low], fs.at[low], ag_send.at[t - 1], ag_recv.at[t - 1], in_plane(t))
        for t in range(1, PLANE)
    ])
    for copy in shares:
        copy.wait_recv()
    next_stage()
    total = fs[...].reshape(rank, 2 * rank)
    counted = jnp.maximum(jnp.sum(jnp.where(spare, total, 0.0), keepdims=True), 1.0)
    twin = jnp.sum(jnp.where((row == 0) & (lane == 1), total, 0.0), keepdims=True)
    total = jnp.where(spare, twin, total)
    for i, inverse in enumerate(inverses(total / counted)):
        if i == 2:
            next_stage()

    zeros = jnp.zeros((rank, 2 * rank), jnp.float32)
    left = exact(inverse, jnp.concatenate([grad, zeros], axis=0))
    precond = exact(left[:rank], inverse) * (1.0 / rank)
    precond = precond + pltpu.roll(precond, rank, 1)
    precond = jnp.where(first[:half], precond[:half], precond[half:])
    next_stage()
    terms = g[...] * precond[None]
    terms = jnp.sum(terms.reshape(n, half // 8, 8, 2 * rank), axis=1).reshape(n * 8, 2 * rank)
    sums = jnp.sum(terms, axis=1, keepdims=True)
    nquery = scores_out.shape[1]
    at = lax.broadcasted_iota(jnp.int32, (n * 8, nquery), 0) // 8
    index = at % high * 8 + at // high % 2 * 4 + at // (2 * high) % 2 * 2 + at // (4 * high)
    scores_out[...] = jnp.sum(jnp.where(index == queries[...], sums, 0.0), axis=0, keepdims=True)
    for copy in started:
        copy.wait_send()


def local(n, hidden, cotangent, loss_mask, project_hidden, project_model, queries):
    _, seq, ff = hidden.shape
    d = cotangent.shape[2]
    rank = project_hidden.shape[1]
    nquery = queries.shape[0]
    high = n // PLANE
    chunks_h, chunks_c = 7, 2
    vmem = pl.BlockSpec(memory_space=pltpu.VMEM)
    hbm = pl.BlockSpec(memory_space=pl.ANY)
    sem = pltpu.SemaphoreType.DMA
    f32 = jnp.float32
    rows = rank // PLANE
    grads, scores = pl.pallas_call(
        functools.partial(kernel, n, chunks_h, chunks_c),
        out_shape=(
            jax.ShapeDtypeStruct((rank // 2, 2 * rank), f32),
            jax.ShapeDtypeStruct((1, nquery), f32),
        ),
        in_specs=[hbm, hbm, vmem, hbm, hbm, vmem],
        out_specs=(vmem, vmem),
        scratch_shapes=[
            pltpu.VMEM((seq, ff), jnp.bfloat16),
            pltpu.VMEM((seq, d), jnp.bfloat16),
            pltpu.VMEM((rank, ff), jnp.bfloat16),
            pltpu.VMEM((rank, d), jnp.bfloat16),
            pltpu.VMEM((rank, 2 * rank), f32),
            pltpu.VMEM((PLANE, rows, 2 * rank), f32),
            pltpu.VMEM((PLANE - 1, rows, 2 * rank), f32),
            pltpu.VMEM((rows, 2 * rank), f32),
            pltpu.VMEM((high - 1, rows, 2 * rank), f32),
            pltpu.VMEM((PLANE, rows, 2 * rank), f32),
            pltpu.VMEM((n, rank // 2, 2 * rank), f32),
            sem((2 * (chunks_h + chunks_c),)),
            sem((PLANE - 1,)),
            sem((PLANE - 1,)),
            sem((high - 1,)),
            sem((high - 1,)),
            sem((PLANE - 1,)),
            sem((PLANE - 1,)),
            sem((high + 2,)),
            sem((high + 2,)),
        ],
        compiler_params=pltpu.CompilerParams(
            collective_id=0, has_side_effects=True, vmem_limit_bytes=48 * 2**20
        ),
    )(hidden, cotangent, loss_mask, project_hidden.T, project_model.T, queries.reshape(1, nquery))
    return grads.reshape(1, rank * rank), scores


def solution(mesh):
    in_specs = (
        P(("groups", "sample"), None, None),
        P(("groups", "sample"), None, None),
        P(("groups", "sample"), None),
        P(),
        P(),
        P("groups"),
    )
    out_specs = (P(("groups", "sample"), None), P(("groups", "sample"), None))
    return jax.shard_map(
        functools.partial(local, mesh.shape["sample"]),
        mesh=mesh, in_specs=in_specs, out_specs=out_specs, check_vma=False,
    )
```

```python
import functools

import jax
import jax.numpy as jnp
from jax import lax
from jax.experimental import pallas as pl
from jax.experimental.pallas import tpu as pltpu
from jax.sharding import PartitionSpec as P

MESH = pl.DeviceIdType.MESH
HIGHEST = lax.Precision.HIGHEST
PLANE = 8
NT = (((1,), (1,)), ((), ()))
SQUARINGS = 7
AHEAD = 4


def exact(a, b):
    return jnp.dot(a, b, precision=HIGHEST, preferred_element_type=jnp.float32)


def inverses(factors):
    rank = factors.shape[0]
    row = lax.broadcasted_iota(jnp.int32, factors.shape, 0)
    lane = lax.broadcasted_iota(jnp.int32, factors.shape, 1)
    first = lane < rank
    diagonal = row == jnp.where(first, lane, lane - rank)

    def both(values):
        one = jnp.sum(jnp.where(first, values, 0.0), keepdims=True)
        two = jnp.sum(jnp.where(first, 0.0, values), keepdims=True)
        lane1 = lax.broadcasted_iota(jnp.int32, (1, 2 * rank), 1)
        return jnp.where(lane1 < rank, one, two)

    trace = both(jnp.where(diagonal, factors, 0.0))
    frob = jnp.sqrt(both(factors * factors))
    lam = 0.1 * trace / rank + 1e-06
    low, high = lam, lam + jnp.minimum(trace, frob) * 1.0001
    damped = jnp.where(diagonal, factors + lam, factors)

    def blocks(values):
        return jnp.concatenate(
            [jnp.where(first, values, 0.0), jnp.where(first, 0.0, values)], axis=0
        )

    eye = blocks(jnp.where(diagonal, 1.0, 0.0))
    damped = blocks(damped)
    scale = 2.0 / (low + high)
    rho = (high - low) / (high + low)
    x = eye * scale
    r = eye - damped * scale
    for _ in range(SQUARINGS):
        c = 2.0 / (2.0 - rho * rho)
        product = exact(jnp.concatenate([r, x], axis=0), r)
        x = (x + product[2 * rank :]) * c
        r = (1.0 - c) * eye + product[: 2 * rank] * c
        rho = rho * rho / (2.0 - rho * rho)
        yield None
    x = x + exact(x, eye - exact(damped, x))
    yield x


def kernel(
    n, chunks_h, chunks_c,
    hidden, cot, mask, proj_h, proj_m, queries,
    grads_out, scores_out,
    h_v, c_v, ph_v, pm_v, m_v, q_v, pair, fac, rs, red, zr, fs, g_a, g_b,
    in_sem, rs_send, rs_recv, z_send, z_recv, ag_send, ag_recv, g_send, g_recv,
):
    seq, ff = h_v.shape
    d = c_v.shape[1]
    rank = ph_v.shape[0]
    me = lax.axis_index("sample")
    high = n // PLANE
    hi, low = me // PLANE, me % PLANE

    def in_plane(t):
        return hi * PLANE + (low + t) % PLANE

    def in_column(t):
        return (hi + t) % high * PLANE + low

    loads = []
    step = d // chunks_c
    for i in range(chunks_c):
        cols = pl.ds(i * step, step)
        loads.append([(cot.at[0, :, cols], c_v.at[:, cols]), (proj_m.at[:, cols], pm_v.at[:, cols])])
    step = ff // chunks_h
    for i in range(chunks_h):
        cols = pl.ds(i * step, step)
        loads.append([(hidden.at[0, :, cols], h_v.at[:, cols]), (proj_h.at[:, cols], ph_v.at[:, cols])])
    copies = []
    for i, two in enumerate(loads):
        copies.append(
            [pltpu.make_async_copy(src, dst, in_sem.at[2 * i + j]) for j, (src, dst) in enumerate(two)]
        )
    small = [
        pltpu.make_async_copy(mask, m_v, in_sem.at[2 * len(loads)]),
        pltpu.make_async_copy(queries, q_v, in_sem.at[2 * len(loads) + 1]),
    ]

    def fetch(i):
        for copy in copies[i] if i < len(loads) else ():
            copy.start()

    def arrived(i):
        for copy in copies[i]:
            copy.wait()
        fetch(i + AHEAD)

    for i in range(AHEAD):
        fetch(i)
    for copy in small:
        copy.start()

    barrier = pltpu.get_barrier_semaphore()
    partners = [in_plane(t) for t in range(1, PLANE)] + [in_column(t) for t in range(1, high)]
    for partner in partners:
        pl.semaphore_signal(barrier, inc=1, device_id={"sample": partner}, device_id_type=MESH)

    weighted = jnp.zeros((rank, seq), jnp.float32)
    step = d // chunks_c
    for i in range(chunks_c):
        arrived(i)
        cols = pl.ds(i * step, step)
        weighted += lax.dot_general(pm_v[:, cols], c_v[:, cols], NT, preferred_element_type=jnp.float32)
    hidden_low = jnp.zeros((rank, seq), jnp.float32)
    step = ff // chunks_h
    for i in range(chunks_h):
        arrived(chunks_c + i)
        cols = pl.ds(i * step, step)
        hidden_low += lax.dot_general(ph_v[:, cols], h_v[:, cols], NT, preferred_element_type=jnp.float32)

    for copy in small:
        copy.wait()
    maskf = m_v[...].astype(jnp.float32)
    both = jnp.concatenate([hidden_low, weighted], axis=0) * maskf
    gram = lax.dot_general(both, both, NT, precision=HIGHEST, preferred_element_type=jnp.float32)
    row = lax.broadcasted_iota(jnp.int32, (rank, 2 * rank), 0)
    lane = lax.broadcasted_iota(jnp.int32, (rank, 2 * rank), 1)
    first = lane < rank
    factors = jnp.where(first, gram[:rank], gram[rank:])
    spare = (row == 1) & (lane == 0)
    count = jnp.sum(maskf, keepdims=True)
    fac[...] = jnp.where(spare, count, factors).reshape(fac.shape)

    pl.semaphore_wait(barrier, len(partners))

    def remote(src, dst, send, recv, partner):
        return pltpu.make_async_remote_copy(
            src_ref=src, dst_ref=dst, send_sem=send, recv_sem=recv,
            device_id={"sample": partner}, device_id_type=MESH,
        )

    started = []

    def start(copies):
        for copy in copies:
            copy.start()
        started.extend(copies)
        return copies

    to_plane = start([
        remote(fac.at[(low + t) % PLANE], rs.at[t - 1], rs_send.at[t - 1], rs_recv.at[t - 1], in_plane(t))
        for t in range(1, PLANE)
    ])

    grad = jnp.where(first, 0.0, gram[:rank]) * (1.0 / seq**0.5)
    twice = grad + pltpu.roll(grad, rank, 1)
    half = rank // 2
    folded = jnp.where(first[:half], twice[:half], twice[half:])
    b4, b2, b1 = low // 4 % 2, low // 2 % 2, low % 2
    place_a = hi + high * (b4 + 2 * b2 + 4 * b1)
    place_b = hi + high * (b2 + 2 * b4 + 4 * b1)
    g_a[place_a] = folded[: half // 2]
    g_b[place_b] = folded[half // 2 :]
    halves = ((g_a, place_a, (4, 2, 1)), (g_b, place_b, (2, 4, 1)))

    def g_copies(stage):
        result = []
        for k, (g, place, bits) in enumerate(halves):
            if stage == 0:
                for t in range(1, high):
                    result.append(
                        remote(g.at[place], g.at[place], g_send.at[k, t - 1], g_recv.at[k, t - 1], in_column(t))
                    )
                continue
            held = high * 2 ** (stage - 1)
            bit = bits[stage - 1]
            partner = me + (1 - 2 * ((me // bit) % 2)) * bit
            span = pl.ds(pl.multiple_of(place // held * held, held), held)
            sem = high - 2 + stage
            result.append(remote(g.at[span], g.at[span], g_send.at[k, sem], g_recv.at[k, sem], partner))
        return result

    stages = [start(g_copies(0))]

    def next_stage():
        for copy in stages[-1]:
            copy.wait_recv()
        if len(stages) < 4:
            stages.append(start(g_copies(len(stages))))

    pair[...] = twice
    grads_out[...] = jnp.where(
        first[:half], pair[pl.ds(0, half, stride=2), :], pair[pl.ds(1, half, stride=2), :]
    )

    for copy in to_plane:
        copy.wait_recv()
    part = fac[low]
    for t in range(PLANE - 1):
        part += rs[t]
    red[...] = part
    to_column = start([
        remote(red, zr.at[t - 1], z_send.at[t - 1], z_recv.at[t - 1], in_column(t))
        for t in range(1, high)
    ])
    for copy in to_column:
        copy.wait_recv()
    for t in range(high - 1):
        part += zr[t]
    fs[low] = part
    shares = start([
        remote(fs.at[low], fs.at[low], ag_send.at[t - 1], ag_recv.at[t - 1], in_plane(t))
        for t in range(1, PLANE)
    ])
    next_stage()
    for copy in shares:
        copy.wait_recv()
    next_stage()
    total = fs[...].reshape(rank, 2 * rank)
    counted = jnp.maximum(jnp.sum(jnp.where(spare, total, 0.0), keepdims=True), 1.0)
    twin = jnp.sum(jnp.where((row == 0) & (lane == 1), total, 0.0), keepdims=True)
    total = jnp.where(spare, twin, total)
    for i, inverse in enumerate(inverses(total / counted)):
        if i == 5:
            next_stage()

    zeros = jnp.zeros((rank, 2 * rank), jnp.float32)
    left = exact(inverse, jnp.concatenate([grad, zeros], axis=0))
    precond = exact(left[:rank], inverse) * (1.0 / rank)
    precond = precond + pltpu.roll(precond, rank, 1)
    precond = jnp.where(first[:half], precond[:half], precond[half:])
    next_stage()
    def terms(g, part):
        products = g[...] * part[None]
        return jnp.sum(products.reshape(n, half // 16, 8, 2 * rank), axis=1)

    two = terms(g_b, precond[half // 2 :])
    order = (0, 2, 1, 3, 4, 6, 5, 7)
    two = jnp.concatenate([two[k * high : (k + 1) * high] for k in order], axis=0)
    sums = (terms(g_a, precond[: half // 2]) + two).reshape(n * 8, 2 * rank)
    sums = jnp.sum(sums, axis=1, keepdims=True)
    nquery = scores_out.shape[1]
    at = lax.broadcasted_iota(jnp.int32, (n * 8, nquery), 0) // 8
    index = at % high * 8 + at // high % 2 * 4 + at // (2 * high) % 2 * 2 + at // (4 * high)
    scores_out[...] = jnp.sum(jnp.where(index == q_v[...], sums, 0.0), axis=0, keepdims=True)
    for copy in started:
        copy.wait_send()


def local(n, hidden, cotangent, loss_mask, project_hidden, project_model, queries):
    _, seq, ff = hidden.shape
    d = cotangent.shape[2]
    rank = project_hidden.shape[1]
    nquery = queries.shape[0]
    high = n // PLANE
    chunks_h, chunks_c = 7, 2
    vmem = pl.BlockSpec(memory_space=pltpu.VMEM)
    hbm = pl.BlockSpec(memory_space=pl.ANY)
    sem = pltpu.SemaphoreType.DMA
    f32 = jnp.float32
    rows = rank // PLANE
    grads, scores = pl.pallas_call(
        functools.partial(kernel, n, chunks_h, chunks_c),
        out_shape=(
            jax.ShapeDtypeStruct((rank // 2, 2 * rank), f32),
            jax.ShapeDtypeStruct((1, nquery), f32),
        ),
        in_specs=[hbm] * 6,
        out_specs=(vmem, vmem),
        scratch_shapes=[
            pltpu.VMEM((seq, ff), jnp.bfloat16),
            pltpu.VMEM((seq, d), jnp.bfloat16),
            pltpu.VMEM((rank, ff), jnp.bfloat16),
            pltpu.VMEM((rank, d), jnp.bfloat16),
            pltpu.VMEM((1, seq), jnp.int32),
            pltpu.VMEM((1, nquery), jnp.int32),
            pltpu.VMEM((rank, 2 * rank), f32),
            pltpu.VMEM((PLANE, rows, 2 * rank), f32),
            pltpu.VMEM((PLANE - 1, rows, 2 * rank), f32),
            pltpu.VMEM((rows, 2 * rank), f32),
            pltpu.VMEM((high - 1, rows, 2 * rank), f32),
            pltpu.VMEM((PLANE, rows, 2 * rank), f32),
            pltpu.VMEM((n, rank // 4, 2 * rank), f32),
            pltpu.VMEM((n, rank // 4, 2 * rank), f32),
            sem((2 * (chunks_h + chunks_c) + 2,)),
            sem((PLANE - 1,)),
            sem((PLANE - 1,)),
            sem((high - 1,)),
            sem((high - 1,)),
            sem((PLANE - 1,)),
            sem((PLANE - 1,)),
            sem((2, high + 2)),
            sem((2, high + 2)),
        ],
        compiler_params=pltpu.CompilerParams(
            collective_id=0, has_side_effects=True, vmem_limit_bytes=63 * 2**20
        ),
    )(hidden, cotangent, loss_mask, project_hidden.T, project_model.T, queries.reshape(1, nquery))
    return grads.reshape(1, rank * rank), scores


def solution(mesh):
    in_specs = (
        P(("groups", "sample"), None, None),
        P(("groups", "sample"), None, None),
        P(("groups", "sample"), None),
        P(),
        P(),
        P("groups"),
    )
    out_specs = (P(("groups", "sample"), None), P(("groups", "sample"), None))
    return jax.shard_map(
        functools.partial(local, mesh.shape["sample"]),
        mesh=mesh, in_specs=in_specs, out_specs=out_specs, check_vma=False,
    )
```

```python
import functools

import jax
import jax.numpy as jnp
from jax import lax
from jax.experimental import pallas as pl
from jax.experimental.pallas import tpu as pltpu
from jax.sharding import PartitionSpec as P

MESH = pl.DeviceIdType.MESH
HIGHEST = lax.Precision.HIGHEST
PLANE = 8
NT = (((1,), (1,)), ((), ()))
SQUARINGS = 7
AHEAD = 4


def exact(a, b):
    return jnp.dot(a, b, precision=HIGHEST, preferred_element_type=jnp.float32)


def inverses(factors):
    rank = factors.shape[0]
    row = lax.broadcasted_iota(jnp.int32, factors.shape, 0)
    lane = lax.broadcasted_iota(jnp.int32, factors.shape, 1)
    first = lane < rank
    diagonal = row == jnp.where(first, lane, lane - rank)

    def both(values):
        one = jnp.sum(jnp.where(first, values, 0.0), keepdims=True)
        two = jnp.sum(jnp.where(first, 0.0, values), keepdims=True)
        lane1 = lax.broadcasted_iota(jnp.int32, (1, 2 * rank), 1)
        return jnp.where(lane1 < rank, one, two)

    trace = both(jnp.where(diagonal, factors, 0.0))
    frob = jnp.sqrt(both(factors * factors))
    lam = 0.1 * trace / rank + 1e-06
    low, high = lam, lam + jnp.minimum(trace, frob) * 1.0001
    damped = jnp.where(diagonal, factors + lam, factors)

    def blocks(values):
        return jnp.concatenate(
            [jnp.where(first, values, 0.0), jnp.where(first, 0.0, values)], axis=0
        )

    eye = blocks(jnp.where(diagonal, 1.0, 0.0))
    damped = blocks(damped)
    scale = 2.0 / (low + high)
    rho = (high - low) / (high + low)
    x = eye * scale
    r = eye - damped * scale
    for _ in range(SQUARINGS):
        c = 2.0 / (2.0 - rho * rho)
        product = exact(jnp.concatenate([r, x], axis=0), r)
        x = (x + product[2 * rank :]) * c
        r = (1.0 - c) * eye + product[: 2 * rank] * c
        rho = rho * rho / (2.0 - rho * rho)
        yield None
    x = x + exact(x, eye - exact(damped, x))
    yield x


def kernel(
    n, chunks_h, chunks_c,
    hidden, cot, mask, proj_h, proj_m, queries,
    grads_out, scores_out,
    h_v, c_v, ph_v, pm_v, m_v, q_v, pair, fac, rs, red, zr, fs, g_a, g_b,
    in_sem, rs_send, rs_recv, z_send, z_recv, ag_send, ag_recv, g_send, g_recv,
):
    seq, ff = h_v.shape
    d = c_v.shape[1]
    rank = ph_v.shape[0]
    me = lax.axis_index("sample")
    high = n // PLANE
    hi, low = me // PLANE, me % PLANE

    def in_plane(t):
        return hi * PLANE + (low + t) % PLANE

    def in_column(t):
        return (hi + t) % high * PLANE + low

    loads = []
    step = d // chunks_c
    for i in range(chunks_c):
        cols = pl.ds(i * step, step)
        loads.append([(cot.at[0, :, cols], c_v.at[:, cols]), (proj_m.at[:, cols], pm_v.at[:, cols])])
    step = ff // chunks_h
    for i in range(chunks_h):
        cols = pl.ds(i * step, step)
        loads.append([(hidden.at[0, :, cols], h_v.at[:, cols]), (proj_h.at[:, cols], ph_v.at[:, cols])])
    copies = []
    for i, two in enumerate(loads):
        copies.append(
            [pltpu.make_async_copy(src, dst, in_sem.at[2 * i + j]) for j, (src, dst) in enumerate(two)]
        )
    small = [
        pltpu.make_async_copy(mask, m_v, in_sem.at[2 * len(loads)]),
        pltpu.make_async_copy(queries, q_v, in_sem.at[2 * len(loads) + 1]),
    ]

    def fetch(i):
        for copy in copies[i] if i < len(loads) else ():
            copy.start()

    def arrived(i):
        for copy in copies[i]:
            copy.wait()
        fetch(i + AHEAD)

    for i in range(AHEAD):
        fetch(i)
    for copy in small:
        copy.start()

    barrier = pltpu.get_barrier_semaphore()
    partners = [in_plane(t) for t in range(1, PLANE)] + [in_column(t) for t in range(1, high)]
    for partner in partners:
        pl.semaphore_signal(barrier, inc=1, device_id={"sample": partner}, device_id_type=MESH)

    weighted = jnp.zeros((rank, seq), jnp.float32)
    step = d // chunks_c
    for i in range(chunks_c):
        arrived(i)
        cols = pl.ds(i * step, step)
        weighted += lax.dot_general(pm_v[:, cols], c_v[:, cols], NT, preferred_element_type=jnp.float32)
    hidden_low = jnp.zeros((rank, seq), jnp.float32)
    step = ff // chunks_h
    for i in range(chunks_h):
        arrived(chunks_c + i)
        cols = pl.ds(i * step, step)
        hidden_low += lax.dot_general(ph_v[:, cols], h_v[:, cols], NT, preferred_element_type=jnp.float32)

    for copy in small:
        copy.wait()
    maskf = m_v[...].astype(jnp.float32)
    both = jnp.concatenate([hidden_low, weighted], axis=0) * maskf
    gram = lax.dot_general(both, both, NT, precision=HIGHEST, preferred_element_type=jnp.float32)
    row = lax.broadcasted_iota(jnp.int32, (rank, 2 * rank), 0)
    lane = lax.broadcasted_iota(jnp.int32, (rank, 2 * rank), 1)
    first = lane < rank
    factors = jnp.where(first, gram[:rank], gram[rank:])
    spare = (row == 1) & (lane == 0)
    count = jnp.sum(maskf, keepdims=True)
    fac[...] = jnp.where(spare, count, factors).reshape(fac.shape)

    pl.semaphore_wait(barrier, len(partners))

    def remote(src, dst, send, recv, partner):
        return pltpu.make_async_remote_copy(
            src_ref=src, dst_ref=dst, send_sem=send, recv_sem=recv,
            device_id={"sample": partner}, device_id_type=MESH,
        )

    started = []

    def start(copies):
        for copy in copies:
            copy.start()
        started.extend(copies)
        return copies

    to_plane = start([
        remote(fac.at[(low + t) % PLANE], rs.at[t - 1], rs_send.at[t - 1], rs_recv.at[t - 1], in_plane(t))
        for t in range(1, PLANE)
    ])

    grad = jnp.where(first, 0.0, gram[:rank]) * (1.0 / seq**0.5)
    twice = grad + pltpu.roll(grad, rank, 1)
    half = rank // 2
    folded = jnp.where(first[:half], twice[:half], twice[half:])
    b4, b2, b1 = low // 4 % 2, low // 2 % 2, low % 2
    place_a = hi + high * (b4 + 2 * b2 + 4 * b1)
    place_b = hi + high * (b2 + 2 * b4 + 4 * b1)
    g_a[place_a] = folded[: half // 2]
    g_b[place_b] = folded[half // 2 :]
    halves = ((g_a, place_a, (4, 2, 1)), (g_b, place_b, (2, 4, 1)))

    def g_copies(stage):
        result = []
        for k, (g, place, bits) in enumerate(halves):
            if stage == 0:
                for t in range(1, high):
                    result.append(
                        remote(g.at[place], g.at[place], g_send.at[k, t - 1], g_recv.at[k, t - 1], in_column(t))
                    )
                continue
            held = high * 2 ** (stage - 1)
            bit = bits[stage - 1]
            partner = me + (1 - 2 * ((me // bit) % 2)) * bit
            span = pl.ds(pl.multiple_of(place // held * held, held), held)
            sem = high - 2 + stage
            result.append(remote(g.at[span], g.at[span], g_send.at[k, sem], g_recv.at[k, sem], partner))
        return result

    stages = [start(g_copies(0))]

    def next_stage():
        for copy in stages[-1]:
            copy.wait_recv()
        if len(stages) < 4:
            stages.append(start(g_copies(len(stages))))

    pair[...] = twice
    grads_out[...] = jnp.where(
        first[:half], pair[pl.ds(0, half, stride=2), :], pair[pl.ds(1, half, stride=2), :]
    )

    for copy in to_plane:
        copy.wait_recv()
    part = fac[low]
    for t in range(PLANE - 1):
        part += rs[t]
    red[...] = part
    to_column = start([
        remote(red, zr.at[t - 1], z_send.at[t - 1], z_recv.at[t - 1], in_column(t))
        for t in range(1, high)
    ])
    next_stage()
    for copy in to_column:
        copy.wait_recv()
    for t in range(high - 1):
        part += zr[t]
    fs[low] = part
    shares = start([
        remote(fs.at[low], fs.at[low], ag_send.at[t - 1], ag_recv.at[t - 1], in_plane(t))
        for t in range(1, PLANE)
    ])
    for copy in shares:
        copy.wait_recv()
    total = fs[...].reshape(rank, 2 * rank)
    counted = jnp.maximum(jnp.sum(jnp.where(spare, total, 0.0), keepdims=True), 1.0)
    twin = jnp.sum(jnp.where((row == 0) & (lane == 1), total, 0.0), keepdims=True)
    total = jnp.where(spare, twin, total)
    for i, inverse in enumerate(inverses(total / counted)):
        if i in (0, 5):
            next_stage()

    zeros = jnp.zeros((rank, 2 * rank), jnp.float32)
    left = exact(inverse, jnp.concatenate([grad, zeros], axis=0))
    precond = exact(left[:rank], inverse) * (1.0 / rank)
    precond = precond + pltpu.roll(precond, rank, 1)
    precond = jnp.where(first[:half], precond[:half], precond[half:])
    next_stage()
    def terms(g, part):
        products = g[...] * part[None]
        return jnp.sum(products.reshape(n, half // 16, 8, 2 * rank), axis=1)

    two = terms(g_b, precond[half // 2 :])
    order = (0, 2, 1, 3, 4, 6, 5, 7)
    two = jnp.concatenate([two[k * high : (k + 1) * high] for k in order], axis=0)
    sums = (terms(g_a, precond[: half // 2]) + two).reshape(n * 8, 2 * rank)
    sums = jnp.sum(sums, axis=1, keepdims=True)
    nquery = scores_out.shape[1]
    at = lax.broadcasted_iota(jnp.int32, (n * 8, nquery), 0) // 8
    index = at % high * 8 + at // high % 2 * 4 + at // (2 * high) % 2 * 2 + at // (4 * high)
    scores_out[...] = jnp.sum(jnp.where(index == q_v[...], sums, 0.0), axis=0, keepdims=True)
    for copy in started:
        copy.wait_send()


def finish(grads, scores, grads_out, scores_out, sem):
    copies = [
        pltpu.make_async_copy(grads, grads_out, sem.at[0]),
        pltpu.make_async_copy(scores, scores_out, sem.at[1]),
    ]
    for copy in copies:
        copy.start()
    for copy in copies:
        copy.wait()


def local(n, hidden, cotangent, loss_mask, project_hidden, project_model, queries):
    _, seq, ff = hidden.shape
    d = cotangent.shape[2]
    rank = project_hidden.shape[1]
    nquery = queries.shape[0]
    high = n // PLANE
    chunks_h, chunks_c = 7, 2
    vmem = pl.BlockSpec(memory_space=pltpu.VMEM)
    hbm = pl.BlockSpec(memory_space=pl.ANY)
    sem = pltpu.SemaphoreType.DMA
    f32 = jnp.float32
    rows = rank // PLANE
    grads, scores = pl.pallas_call(
        functools.partial(kernel, n, chunks_h, chunks_c),
        out_shape=(
            jax.ShapeDtypeStruct((rank // 2, 2 * rank), f32),
            jax.ShapeDtypeStruct((1, nquery), f32),
        ),
        in_specs=[hbm] * 6,
        out_specs=(vmem, vmem),
        scratch_shapes=[
            pltpu.VMEM((seq, ff), jnp.bfloat16),
            pltpu.VMEM((seq, d), jnp.bfloat16),
            pltpu.VMEM((rank, ff), jnp.bfloat16),
            pltpu.VMEM((rank, d), jnp.bfloat16),
            pltpu.VMEM((1, seq), jnp.int32),
            pltpu.VMEM((1, nquery), jnp.int32),
            pltpu.VMEM((rank, 2 * rank), f32),
            pltpu.VMEM((PLANE, rows, 2 * rank), f32),
            pltpu.VMEM((PLANE - 1, rows, 2 * rank), f32),
            pltpu.VMEM((rows, 2 * rank), f32),
            pltpu.VMEM((high - 1, rows, 2 * rank), f32),
            pltpu.VMEM((PLANE, rows, 2 * rank), f32),
            pltpu.VMEM((n, rank // 4, 2 * rank), f32),
            pltpu.VMEM((n, rank // 4, 2 * rank), f32),
            sem((2 * (chunks_h + chunks_c) + 2,)),
            sem((PLANE - 1,)),
            sem((PLANE - 1,)),
            sem((high - 1,)),
            sem((high - 1,)),
            sem((PLANE - 1,)),
            sem((PLANE - 1,)),
            sem((2, high + 2)),
            sem((2, high + 2)),
        ],
        compiler_params=pltpu.CompilerParams(
            collective_id=0, has_side_effects=True, vmem_limit_bytes=63 * 2**20
        ),
    )(hidden, cotangent, loss_mask, project_hidden.T, project_model.T, queries.reshape(1, nquery))
    grads, scores = pl.pallas_call(
        finish,
        out_shape=(
            jax.ShapeDtypeStruct(grads.shape, f32),
            jax.ShapeDtypeStruct(scores.shape, f32),
        ),
        in_specs=[hbm, hbm],
        out_specs=(hbm, hbm),
        scratch_shapes=[sem((2,))],
        compiler_params=pltpu.CompilerParams(vmem_limit_bytes=63 * 2**20),
    )(grads, scores)
    return grads.reshape(1, rank * rank), scores


def solution(mesh):
    in_specs = (
        P(("groups", "sample"), None, None),
        P(("groups", "sample"), None, None),
        P(("groups", "sample"), None),
        P(),
        P(),
        P("groups"),
    )
    out_specs = (P(("groups", "sample"), None), P(("groups", "sample"), None))
    return jax.shard_map(
        functools.partial(local, mesh.shape["sample"]),
        mesh=mesh, in_specs=in_specs, out_specs=out_specs, check_vma=False,
    )
```

```python
import functools

import jax
import jax.numpy as jnp
from jax import lax
from jax.experimental import pallas as pl
from jax.experimental.pallas import tpu as pltpu
from jax.sharding import PartitionSpec as P

MESH = pl.DeviceIdType.MESH
HIGHEST = lax.Precision.HIGHEST
PLANE = 8
NT = (((1,), (1,)), ((), ()))
SQUARINGS = 7
AHEAD = 4


def exact(a, b):
    return jnp.dot(a, b, precision=HIGHEST, preferred_element_type=jnp.float32)


def inverses(factors):
    rank = factors.shape[0]
    row = lax.broadcasted_iota(jnp.int32, factors.shape, 0)
    lane = lax.broadcasted_iota(jnp.int32, factors.shape, 1)
    first = lane < rank
    diagonal = row == jnp.where(first, lane, lane - rank)

    def both(values):
        one = jnp.sum(jnp.where(first, values, 0.0), keepdims=True)
        two = jnp.sum(jnp.where(first, 0.0, values), keepdims=True)
        lane1 = lax.broadcasted_iota(jnp.int32, (1, 2 * rank), 1)
        return jnp.where(lane1 < rank, one, two)

    trace = both(jnp.where(diagonal, factors, 0.0))
    frob = jnp.sqrt(both(factors * factors))
    lam = 0.1 * trace / rank + 1e-06
    low, high = lam, lam + jnp.minimum(trace, frob) * 1.0001
    damped = jnp.where(diagonal, factors + lam, factors)

    def blocks(values):
        return jnp.concatenate(
            [jnp.where(first, values, 0.0), jnp.where(first, 0.0, values)], axis=0
        )

    eye = blocks(jnp.where(diagonal, 1.0, 0.0))
    damped = blocks(damped)
    scale = 2.0 / (low + high)
    rho = (high - low) / (high + low)
    x = eye * scale
    r = eye - damped * scale
    for _ in range(SQUARINGS):
        c = 2.0 / (2.0 - rho * rho)
        product = exact(jnp.concatenate([r, x], axis=0), r)
        x = (x + product[2 * rank :]) * c
        r = (1.0 - c) * eye + product[: 2 * rank] * c
        rho = rho * rho / (2.0 - rho * rho)
        yield None
    x = x + exact(x, eye - exact(damped, x))
    yield x


def kernel(
    n, chunks_h, chunks_c,
    hidden, cot, mask, proj_h, proj_m, queries,
    grads_out, scores_out,
    h_v, c_v, ph_v, pm_v, m_v, q_v, pair, fac, rs, red, zr, fs, g_a, g_b,
    in_sem, rs_send, rs_recv, z_send, z_recv, ag_send, ag_recv, g_send, g_recv,
):
    seq, ff = h_v.shape
    d = c_v.shape[1]
    rank = ph_v.shape[0]
    me = lax.axis_index("sample")
    high = n // PLANE
    hi, low = me // PLANE, me % PLANE

    def in_plane(t):
        return hi * PLANE + (low + t) % PLANE

    def in_column(t):
        return (hi + t) % high * PLANE + low

    loads = []
    step = d // chunks_c
    for i in range(chunks_c):
        cols = pl.ds(i * step, step)
        loads.append([(cot.at[0, :, cols], c_v.at[:, cols]), (proj_m.at[:, cols], pm_v.at[:, cols])])
    step = ff // chunks_h
    for i in range(chunks_h):
        cols = pl.ds(i * step, step)
        loads.append([(hidden.at[0, :, cols], h_v.at[:, cols]), (proj_h.at[:, cols], ph_v.at[:, cols])])
    copies = []
    for i, two in enumerate(loads):
        copies.append(
            [pltpu.make_async_copy(src, dst, in_sem.at[2 * i + j]) for j, (src, dst) in enumerate(two)]
        )
    small = [
        pltpu.make_async_copy(mask, m_v, in_sem.at[2 * len(loads)]),
        pltpu.make_async_copy(queries, q_v, in_sem.at[2 * len(loads) + 1]),
    ]

    def fetch(i):
        for copy in copies[i] if i < len(loads) else ():
            copy.start()

    def arrived(i):
        for copy in copies[i]:
            copy.wait()
        fetch(i + AHEAD)

    for i in range(AHEAD):
        fetch(i)
    for copy in small:
        copy.start()

    barrier = pltpu.get_barrier_semaphore()
    partners = [in_plane(t) for t in range(1, PLANE)] + [in_column(t) for t in range(1, high)]
    for partner in partners:
        pl.semaphore_signal(barrier, inc=1, device_id={"sample": partner}, device_id_type=MESH)

    weighted = jnp.zeros((rank, seq), jnp.float32)
    step = d // chunks_c
    for i in range(chunks_c):
        arrived(i)
        cols = pl.ds(i * step, step)
        weighted += lax.dot_general(pm_v[:, cols], c_v[:, cols], NT, preferred_element_type=jnp.float32)
    hidden_low = jnp.zeros((rank, seq), jnp.float32)
    step = ff // chunks_h
    for i in range(chunks_h):
        arrived(chunks_c + i)
        cols = pl.ds(i * step, step)
        hidden_low += lax.dot_general(ph_v[:, cols], h_v[:, cols], NT, preferred_element_type=jnp.float32)

    for copy in small:
        copy.wait()
    maskf = m_v[...].astype(jnp.float32)
    both = jnp.concatenate([hidden_low, weighted], axis=0) * maskf
    gram = lax.dot_general(both, both, NT, precision=HIGHEST, preferred_element_type=jnp.float32)
    row = lax.broadcasted_iota(jnp.int32, (rank, 2 * rank), 0)
    lane = lax.broadcasted_iota(jnp.int32, (rank, 2 * rank), 1)
    first = lane < rank
    factors = jnp.where(first, gram[:rank], gram[rank:])
    spare = (row == 1) & (lane == 0)
    count = jnp.sum(maskf, keepdims=True)
    fac[...] = jnp.where(spare, count, factors).reshape(fac.shape)

    pl.semaphore_wait(barrier, len(partners))

    def remote(src, dst, send, recv, partner):
        return pltpu.make_async_remote_copy(
            src_ref=src, dst_ref=dst, send_sem=send, recv_sem=recv,
            device_id={"sample": partner}, device_id_type=MESH,
        )

    started = []

    def start(copies):
        for copy in copies:
            copy.start()
        started.extend(copies)
        return copies

    to_plane = start([
        remote(fac.at[(low + t) % PLANE], rs.at[t - 1], rs_send.at[t - 1], rs_recv.at[t - 1], in_plane(t))
        for t in range(1, PLANE)
    ])

    grad = jnp.where(first, 0.0, gram[:rank]) * (1.0 / seq**0.5)
    twice = grad + pltpu.roll(grad, rank, 1)
    half = rank // 2
    folded = jnp.where(first[:half], twice[:half], twice[half:])
    b4, b2, b1 = low // 4 % 2, low // 2 % 2, low % 2
    place_a = hi + high * (b4 + 2 * b2 + 4 * b1)
    place_b = hi + high * (b2 + 2 * b4 + 4 * b1)
    g_a[place_a] = folded[: half // 2]
    g_b[place_b] = folded[half // 2 :]
    halves = ((g_a, place_a, (4, 2, 1)), (g_b, place_b, (2, 4, 1)))

    def g_copies(stage):
        result = []
        for k, (g, place, bits) in enumerate(halves):
            if stage == 0:
                for t in range(1, high):
                    result.append(
                        remote(g.at[place], g.at[place], g_send.at[k, t - 1], g_recv.at[k, t - 1], in_column(t))
                    )
                continue
            held = high * 2 ** (stage - 1)
            bit = bits[stage - 1]
            partner = me + (1 - 2 * ((me // bit) % 2)) * bit
            span = pl.ds(pl.multiple_of(place // held * held, held), held)
            sem = high - 2 + stage
            result.append(remote(g.at[span], g.at[span], g_send.at[k, sem], g_recv.at[k, sem], partner))
        return result

    stages = [start(g_copies(0))]

    def next_stage():
        for copy in stages[-1]:
            copy.wait_recv()
        if len(stages) < 4:
            stages.append(start(g_copies(len(stages))))

    pair[...] = twice
    grads_out[...] = jnp.where(
        first[:half], pair[pl.ds(0, half, stride=2), :], pair[pl.ds(1, half, stride=2), :]
    )

    for copy in to_plane:
        copy.wait_recv()
    part = fac[low]
    for t in range(PLANE - 1):
        part += rs[t]
    red[...] = part
    to_column = start([
        remote(red, zr.at[t - 1], z_send.at[t - 1], z_recv.at[t - 1], in_column(t))
        for t in range(1, high)
    ])
    for copy in to_column:
        copy.wait_recv()
    for t in range(high - 1):
        part += zr[t]
    fs[low] = part
    shares = start([
        remote(fs.at[low], fs.at[low], ag_send.at[t - 1], ag_recv.at[t - 1], in_plane(t))
        for t in range(1, PLANE)
    ])
    next_stage()
    for copy in shares:
        copy.wait_recv()
    next_stage()
    total = fs[...].reshape(rank, 2 * rank)
    counted = jnp.maximum(jnp.sum(jnp.where(spare, total, 0.0), keepdims=True), 1.0)
    twin = jnp.sum(jnp.where((row == 0) & (lane == 1), total, 0.0), keepdims=True)
    total = jnp.where(spare, twin, total)
    for i, inverse in enumerate(inverses(total / counted)):
        if i == 5:
            next_stage()

    zeros = jnp.zeros((rank, 2 * rank), jnp.float32)
    left = exact(inverse, jnp.concatenate([grad, zeros], axis=0))
    precond = exact(left[:rank], inverse) * (1.0 / rank)
    precond = precond + pltpu.roll(precond, rank, 1)
    precond = jnp.where(first[:half], precond[:half], precond[half:])
    next_stage()
    def terms(g, part):
        products = g[...] * part[None]
        return jnp.sum(products.reshape(n, half // 16, 8, 2 * rank), axis=1)

    two = terms(g_b, precond[half // 2 :])
    order = (0, 2, 1, 3, 4, 6, 5, 7)
    two = jnp.concatenate([two[k * high : (k + 1) * high] for k in order], axis=0)
    sums = (terms(g_a, precond[: half // 2]) + two).reshape(n * 8, 2 * rank)
    sums = jnp.sum(sums, axis=1, keepdims=True)
    nquery = scores_out.shape[1]
    at = lax.broadcasted_iota(jnp.int32, (n * 8, nquery), 0) // 8
    index = at % high * 8 + at // high % 2 * 4 + at // (2 * high) % 2 * 2 + at // (4 * high)
    scores_out[...] = jnp.sum(jnp.where(index == q_v[...], sums, 0.0), axis=0, keepdims=True)
    for copy in started:
        copy.wait_send()


def finish(grads, scores, grads_out, scores_out, sem):
    copies = [
        pltpu.make_async_copy(grads, grads_out, sem.at[0]),
        pltpu.make_async_copy(scores, scores_out, sem.at[1]),
    ]
    for copy in copies:
        copy.start()
    for copy in copies:
        copy.wait()


def local(n, hidden, cotangent, loss_mask, project_hidden, project_model, queries):
    _, seq, ff = hidden.shape
    d = cotangent.shape[2]
    rank = project_hidden.shape[1]
    nquery = queries.shape[0]
    high = n // PLANE
    chunks_h, chunks_c = 7, 2
    vmem = pl.BlockSpec(memory_space=pltpu.VMEM)
    hbm = pl.BlockSpec(memory_space=pl.ANY)
    sem = pltpu.SemaphoreType.DMA
    f32 = jnp.float32
    rows = rank // PLANE
    grads, scores = pl.pallas_call(
        functools.partial(kernel, n, chunks_h, chunks_c),
        out_shape=(
            jax.ShapeDtypeStruct((rank // 2, 2 * rank), f32),
            jax.ShapeDtypeStruct((1, nquery), f32),
        ),
        in_specs=[hbm] * 6,
        out_specs=(vmem, vmem),
        scratch_shapes=[
            pltpu.VMEM((seq, ff), jnp.bfloat16),
            pltpu.VMEM((seq, d), jnp.bfloat16),
            pltpu.VMEM((rank, ff), jnp.bfloat16),
            pltpu.VMEM((rank, d), jnp.bfloat16),
            pltpu.VMEM((1, seq), jnp.int32),
            pltpu.VMEM((1, nquery), jnp.int32),
            pltpu.VMEM((rank, 2 * rank), f32),
            pltpu.VMEM((PLANE, rows, 2 * rank), f32),
            pltpu.VMEM((PLANE - 1, rows, 2 * rank), f32),
            pltpu.VMEM((rows, 2 * rank), f32),
            pltpu.VMEM((high - 1, rows, 2 * rank), f32),
            pltpu.VMEM((PLANE, rows, 2 * rank), f32),
            pltpu.VMEM((n, rank // 4, 2 * rank), f32),
            pltpu.VMEM((n, rank // 4, 2 * rank), f32),
            sem((2 * (chunks_h + chunks_c) + 2,)),
            sem((PLANE - 1,)),
            sem((PLANE - 1,)),
            sem((high - 1,)),
            sem((high - 1,)),
            sem((PLANE - 1,)),
            sem((PLANE - 1,)),
            sem((2, high + 2)),
            sem((2, high + 2)),
        ],
        compiler_params=pltpu.CompilerParams(
            collective_id=0, has_side_effects=True, vmem_limit_bytes=63 * 2**20
        ),
    )(hidden, cotangent, loss_mask, project_hidden.T, project_model.T, queries.reshape(1, nquery))
    grads, scores = pl.pallas_call(
        finish,
        out_shape=(
            jax.ShapeDtypeStruct(grads.shape, f32),
            jax.ShapeDtypeStruct(scores.shape, f32),
        ),
        in_specs=[hbm, hbm],
        out_specs=(hbm, hbm),
        scratch_shapes=[sem((2,))],
        compiler_params=pltpu.CompilerParams(vmem_limit_bytes=63 * 2**20),
    )(grads, scores)
    return grads.reshape(1, rank * rank), scores


def solution(mesh):
    in_specs = (
        P(("groups", "sample"), None, None),
        P(("groups", "sample"), None, None),
        P(("groups", "sample"), None),
        P(),
        P(),
        P("groups"),
    )
    out_specs = (P(("groups", "sample"), None), P(("groups", "sample"), None))
    return jax.shard_map(
        functools.partial(local, mesh.shape["sample"]),
        mesh=mesh, in_specs=in_specs, out_specs=out_specs, check_vma=False,
    )
```
